512 devices in a mesh: row: 16 (over y_hi, x), col: 32 (over y_lo, z, core).
Axes of the slice: x: 4, y: 8 (y_hi: 4, y_lo: 2; y = y_hi * 2 + y_lo), z: 8, core: 2. Of those that a mesh axis runs over, the one named last changes fastest.
Arguments:
- tokens: bfloat16 [256, 12288], P('col', 'row'), may hold values from -6 to 6
- cotangent: bfloat16 [256, 12288], P('col', 'row'), may hold values from -3 to 3
- weight_in: bfloat16 [12288, 24576], P('row', 'col'), may hold values from -0.0546875 to 0.0546875
- weight_out: bfloat16 [24576, 12288], P('col', 'row'), may hold values from -0.0390625 to 0.0390625
Outputs:
- mixed: bfloat16 [256, 12288], P('col', 'row')
- grad_tokens: bfloat16 [256, 12288], P('col', 'row')
- grad_in: bfloat16 [12288, 24576], P('row', 'col')
- grad_out: bfloat16 [24576, 12288], P('col', 'row')
The draws below stay inside these ranges and needn't reach their ends.
All inputs are finite; a program needn't handle non-finite values.
Results may differ from the reference program's by a relative error of at most 0.0049.
Values may be sent and summed in bfloat16 or wider, within the bound.
A program may use at most 64 MiB of HBM per device.

```python
import jax
import jax.numpy as jnp
from jax import lax

D = 12288
FF = 24576
TOKENS = 256


def shard_levels(key, shape, split, smallest, top_value):
    def one(position, blocks):
        steps = jax.random.uniform(jax.random.fold_in(jax.random.fold_in(key, 6), position), (blocks,), jnp.float32, smallest / len(split), top_value / len(split))
        return jnp.repeat(jnp.exp(steps), shape[position] // blocks).reshape((-1,) + (1,) * (len(shape) - position - 1))

    loudness = one(*split[0])
    for cut in split[1:]:
        loudness = loudness * one(*cut)
    return loudness


def gaussian(stream_key, dims, deviation, bound, split=(), held_as=jnp.bfloat16):
    values = jax.random.normal(stream_key, dims, jnp.float32) * deviation
    if len(split) > 0:
        values = shard_levels(stream_key, dims, split, -0.22, 0.18) * values
    return jnp.clip(values, min=-bound, max=bound).astype(held_as)


def setup_inputs(seed: int = 0) -> dict:
    key_list = jax.random.split(jax.random.key(seed), 5)
    tokens = gaussian(key_list[0], (TOKENS, D), 1.0, 6.0, ((0, 32), (1, 16)))
    cotangent = gaussian(key_list[1], (TOKENS, D), 0.5, 3.0, ((0, 32), (1, 16)))
    weight_in = gaussian(key_list[2], (D, FF), D ** -0.5, 0.0546875, ((0, 16), (1, 32)))
    weight_out = gaussian(key_list[3], (FF, D), FF ** -0.5, 0.0390625, ((0, 32), (1, 16)))
    return {"tokens": tokens, "cotangent": cotangent, "weight_in": weight_in, "weight_out": weight_out}


def gelu_parts(pre_act):
    normal_cdf = 0.5 * (1.0 + jax.scipy.special.erf(pre_act * 0.7071067811865476))
    density = jnp.exp(-0.5 * pre_act * pre_act) * 0.3989422804014327
    return pre_act * normal_cdf, normal_cdf + pre_act * density


def contract_first(left_side, right_side):
    return lax.dot_general(left_side, right_side, (((0,), (0,)), ((), ())), preferred_element_type=jnp.float32)


def contract_last(left_side, right_side):
    return lax.dot_general(left_side, right_side, (((1,), (1,)), ((), ())), preferred_element_type=jnp.float32)


def reference(tokens, cotangent, weight_in, weight_out):
    pre_act = jnp.dot(tokens, weight_in, preferred_element_type=jnp.float32)
    gelu_value, gelu_slope = gelu_parts(pre_act)
    hidden = gelu_value.astype(jnp.bfloat16)
    mixed = jnp.dot(hidden, weight_out, preferred_element_type=jnp.float32).astype(jnp.bfloat16)
    grad_hidden = contract_last(cotangent, weight_out)
    grad_pre = (grad_hidden * gelu_slope).astype(jnp.bfloat16)
    grad_in = contract_first(tokens, grad_pre).astype(jnp.bfloat16)
    grad_out = contract_first(hidden, cotangent).astype(jnp.bfloat16)
    grad_tokens = contract_last(grad_pre, weight_in).astype(jnp.bfloat16)
    return (mixed, grad_tokens, grad_in, grad_out)
```

```python
import jax
import jax.numpy as jnp
from jax import lax
from jax.experimental import pallas as pl
from jax.experimental.pallas import tpu as pltpu
from jax.sharding import PartitionSpec as P

MESH = pl.DeviceIdType.MESH
BF16, F32 = jnp.bfloat16, jnp.float32
NX, NY, NP, NZ, NK = 4, 4, 2, 8, 2
Z_ORDER = (2, 6, 1, 5, 3, 7, 4)


def gelu_parts(pre_act):
    normal_cdf = 0.5 * (1.0 + jax.scipy.special.erf(pre_act * 0.7071067811865476))
    density = jnp.exp(-0.5 * pre_act * pre_act) * 0.3989422804014327
    return pre_act * normal_cdf, normal_cdf + pre_act * density


def dot(left, right, dims):
    return lax.dot_general(left, right, (dims, ((), ())), preferred_element_type=F32)


def kernel(
    tok_ref, cot_ref, wi_hbm, wo_hbm,
    mixed_ref, gt_ref, gi_hbm, go_hbm,
    wi, wo, gat, tok, cot, own, xs, xr, ys, yr, act,
    part, ss, sr, ps, pr, zs, zr, gi, go,
    w_sem, g_sem,
    az_s, az_r, ay_s, ay_r, ak_s, ak_r,
    rx_s, rx_r, ry_s, ry_r,
    cy_s, cy_r, cx_s, cx_r,
    dk_s, dk_r, dy_s, dy_r, dz_s, dz_r,
):
    r, c = lax.axis_index("row"), lax.axis_index("col")
    yh, x = r // NX, lax.rem(r, NX)
    p, z, k = c // (NZ * NK), lax.rem(c // NK, NZ), lax.rem(c, NK)
    nk, np_ = 1 - k, 1 - p

    def col_dev(p_, z_, k_):
        return (r, p_ * (NZ * NK) + z_ * NK + k_)

    def row_dev(yh_, x_):
        return (yh_ * NX + x_, c)

    def add(a, d, n):
        return lax.rem(a + d + n, n)

    x_dev = [row_dev(yh, add(x, d, NX)) for d in range(NX)]
    y_dev = [row_dev(add(yh, d, NY), x) for d in range(NY)]
    z_dev = [col_dev(p, add(z, d, NZ), k) for d in range(NZ)]
    p_dev, k_dev = col_dev(np_, z, k), col_dev(p, z, nk)

    def copy(src, dst, s_sem, r_sem, device):
        return pltpu.make_async_remote_copy(
            src_ref=src, dst_ref=dst, send_sem=s_sem, recv_sem=r_sem,
            device_id=device, device_id_type=MESH,
        )

    load_wi = pltpu.make_async_copy(wi_hbm, wi, w_sem.at[0])
    load_wo = pltpu.make_async_copy(wo_hbm, wo, w_sem.at[1])
    load_wi.start()
    load_wo.start()

    peers = x_dev[1:] + y_dev[1:] + z_dev[1:] + [p_dev, k_dev]
    barrier = pltpu.get_barrier_semaphore()
    for peer in peers:
        pl.semaphore_signal(barrier, inc=1, device_id=peer, device_id_type=MESH)
    q_me = p * NZ + z
    gat[k, q_me] = jnp.concatenate(
        [tok_ref[...].astype(F32), cot_ref[...].astype(F32)], axis=0
    ).astype(BF16)
    pl.semaphore_wait(barrier, len(peers))

    sends = []

    def start(*args):
        one = copy(*args)
        one.start()
        sends.append(one)

    def gat_at(k_, p_, d):
        return gat.at[k_, p_ * NZ + add(z, -d, NZ)]

    def z_copy(d):
        return copy(gat.at[k, q_me], gat.at[k, q_me], az_s.at[d], az_r.at[d], z_dev[d])

    def z_arrived(d):
        blk = gat_at(k, p, d)
        copy(blk, blk, az_s.at[d], az_r.at[d], z_dev[d]).wait_recv()

    def forward(d):
        blk = gat_at(k, p, d)
        start(blk, blk, ay_s.at[d], ay_r.at[d], p_dev)
        start(blk, blk, ak_s.at[0, d], ak_r.at[0, d], k_dev)

    def forward_pair(d):
        blk = gat_at(k, np_, d)
        copy(blk, blk, ay_s.at[d], ay_r.at[d], p_dev).wait_recv()
        start(blk, blk, ak_s.at[1, d], ak_r.at[1, d], k_dev)

    def core_arrived(d):
        for side, p_ in ((0, p), (1, np_)):
            blk = gat_at(nk, p_, d)
            copy(blk, blk, ak_s.at[side, d], ak_r.at[side, d], k_dev).wait_recv()

    for d in Z_ORDER:
        one = z_copy(d)
        one.start()
        sends.append(one)
    forward(0)

    def row_terms(d0):
        core_arrived(d0)
        core_arrived(d0 + 4)
        xt = lax.rem(z - d0 + NZ, NX)
        for j in range(NY):
            q = j * NX + xt
            one, two = gat[0, q].astype(F32), gat[1, q].astype(F32)
            tok[xt, pl.ds(16 * j, 16), :] = jnp.concatenate([one[:8], two[:8]], 0).astype(BF16)
            cot[xt, pl.ds(16 * j, 16), :] = jnp.concatenate([one[8:], two[8:]], 0).astype(BF16)
        dx = lax.rem(xt - x + NX, NX)
        for s in range(2):
            if s == 0:
                term = dot(tok[xt], wi[...], ((1,), (0,)))
            else:
                term = dot(cot[xt], wo[...], ((1,), (1,)))

            @pl.when(dx == 0)
            def _():
                own[s] = term.reshape(NY, 16, 768)

            @pl.when(dx != 0)
            def _():
                xs[xt, s] = term.astype(BF16).reshape(NY, 16, 768)
                copy(
                    xs.at[xt, s], xr.at[dx, s], rx_s.at[dx, s], rx_r.at[dx, s],
                    row_dev(yh, xt),
                ).start()

    z_arrived(2)
    forward(2)
    z_arrived(6)
    forward(6)
    forward_pair(0)
    z_arrived(1)
    forward(1)
    forward_pair(2)
    z_arrived(5)
    forward(5)
    forward_pair(6)
    load_wi.wait()
    load_wo.wait()
    row_terms(2)
    forward_pair(1)
    z_arrived(3)
    forward(3)
    forward_pair(5)
    z_arrived(7)
    forward(7)
    row_terms(1)
    forward_pair(3)
    z_arrived(4)
    forward(4)
    forward_pair(7)
    forward_pair(4)
    row_terms(3)
    row_terms(0)

    for d in range(1, NX):
        for s in range(2):
            one = copy(xs.at[0, s], xr.at[d, s], rx_s.at[d, s], rx_r.at[d, s], x_dev[d])
            one.wait_recv()
            one.wait_send()

    def x_sum(j, s):
        return (
            own[s, j] + xr[1, s, j].astype(F32) + xr[2, s, j].astype(F32) + xr[3, s, j].astype(F32)
        )

    for d in (2, 1, 3):
        j = add(yh, d, NY)
        for s in range(2):
            ys[d, s] = x_sum(j, s).astype(BF16)
        start(ys.at[d], yr.at[d], ry_s.at[d], ry_r.at[d], y_dev[d])
    sums = [x_sum(yh, s) for s in range(2)]
    for d in (1, 3, 2):
        copy(ys.at[d], yr.at[d], ry_s.at[d], ry_r.at[d], y_dev[d]).wait_recv()
        sums = [sums[s] + yr[d, s].astype(F32) for s in range(2)]
    value, slope = gelu_parts(sums[0])
    act[x, yh, 0] = value.astype(BF16)
    act[x, yh, 1] = (sums[1] * slope).astype(BF16)

    mine = act.at[x, yh]
    for d in (2, 1, 3):
        start(mine, mine, cy_s.at[d], cy_r.at[d], y_dev[d])
    for d in (0, 1, 3, 2):
        blk = act.at[x, add(yh, -d, NY)]
        if d:
            copy(blk, blk, cy_s.at[d], cy_r.at[d], y_dev[d]).wait_recv()
        for e in (2, 1, 3):
            start(blk, blk, cx_s.at[d, e], cx_r.at[d, e], x_dev[e])

    for e in (0, 1, 3, 2):
        xt = add(x, -e, NX)
        if e:
            for d in (0, 1, 3, 2):
                blk = act.at[xt, add(yh, -d, NY)]
                copy(blk, blk, cx_s.at[d, e], cx_r.at[d, e], x_dev[e]).wait_recv()
        mix = dot(act[xt, :, 0].reshape(64, 768), wo[...], ((1,), (0,)))
        gtk = dot(act[xt, :, 1].reshape(64, 768), wi[...], ((1,), (1,)))
        for j in range(NY):
            two = [
                jnp.concatenate([mix[16 * j + 8 * i:16 * j + 8 * i + 8], gtk[16 * j + 8 * i:16 * j + 8 * i + 8]], 0)
                for i in range(2)
            ]
            part[e, j] = jnp.where(k == 0, two[0], two[1])
            ss[e, j] = jnp.where(k == 0, two[1], two[0])
        start(ss.at[e], sr.at[e], dk_s.at[e], dk_r.at[e], k_dev)

    def grad(left, right, out, hbm, sem):
        for m in range(3):
            cols = pl.ds(256 * m, 256)
            out[:, cols] = dot(left, right[:, 256 * m:256 * m + 256], ((0,), (0,))).astype(BF16)
        pltpu.make_async_copy(out, hbm, sem).start()

    for e in (0, 1, 3, 2):
        copy(ss.at[e], sr.at[e], dk_s.at[e], dk_r.at[e], k_dev).wait_recv()
        for i in range(2):
            j = 2 * np_ + i
            ps[e, i] = (part[e, j] + sr[e, j]).astype(BF16)
        start(ps.at[e], pr.at[e], dy_s.at[e], dy_r.at[e], p_dev)

    grad(tok[...].reshape(256, 768), act[:, :, 1].reshape(256, 768), gi, gi_hbm, g_sem.at[0])

    for e in (0, 1, 3, 2):
        copy(ps.at[e], pr.at[e], dy_s.at[e], dy_r.at[e], p_dev).wait_recv()
        for i in range(2):
            j = 2 * p + i
            zt = NX * i + add(x, -e, NX)
            total = part[e, j] + sr[e, j] + pr[e, i].astype(F32)
            dz = lax.rem(zt - z + NZ, NZ)

            @pl.when(dz == 0)
            def _():
                part[0, 2 * np_] = total

            @pl.when(dz != 0)
            def _():
                zs[dz] = total.astype(BF16)
                copy(
                    zs.at[dz], zr.at[dz], dz_s.at[dz], dz_r.at[dz], col_dev(p, zt, k)
                ).start()

    grad(act[:, :, 0].reshape(256, 768), cot[...].reshape(256, 768), go, go_hbm, g_sem.at[1])

    total = part[0, 2 * np_]
    for d in range(1, NZ):
        one = copy(zs.at[d], zr.at[d], dz_s.at[d], dz_r.at[d], z_dev[d])
        one.wait_recv()
        one.wait_send()
        total = total + zr[d].astype(F32)
    mixed_ref[...] = total[:8].astype(BF16)
    gt_ref[...] = total[8:].astype(BF16)

    for one in sends:
        one.wait_send()
    pltpu.make_async_copy(gi, gi_hbm, g_sem.at[0]).wait()
    pltpu.make_async_copy(go, go_hbm, g_sem.at[1]).wait()


def shards(tokens, cotangent, weight_in, weight_out):
    dma = pltpu.SemaphoreType.DMA
    vmem, hbm = pl.BlockSpec(memory_space=pltpu.VMEM), pl.BlockSpec(memory_space=pl.ANY)
    shape = lambda a: jax.ShapeDtypeStruct(a.shape, BF16)
    sem = lambda *n: [dma(n), dma(n)]
    return pl.pallas_call(
        kernel,
        out_shape=(shape(tokens), shape(tokens), shape(weight_in), shape(weight_out)),
        in_specs=[vmem, vmem, hbm, hbm],
        out_specs=(vmem, vmem, hbm, hbm),
        scratch_shapes=[
            pltpu.VMEM((768, 768), BF16),
            pltpu.VMEM((768, 768), BF16),
            pltpu.VMEM((NK, NP * NZ, 16, 768), BF16),
            pltpu.VMEM((NX, 64, 768), BF16),
            pltpu.VMEM((NX, 64, 768), BF16),
            pltpu.VMEM((2, NY, 16, 768), F32),
            pltpu.VMEM((NX, 2, NY, 16, 768), BF16),
            pltpu.VMEM((NX, 2, NY, 16, 768), BF16),
            pltpu.VMEM((NY, 2, 16, 768), BF16),
            pltpu.VMEM((NY, 2, 16, 768), BF16),
            pltpu.VMEM((NX, NY, 2, 16, 768), BF16),
            pltpu.VMEM((NX, NY, 16, 768), F32),
            pltpu.VMEM((NX, NY, 16, 768), F32),
            pltpu.VMEM((NX, NY, 16, 768), F32),
            pltpu.VMEM((NX, 2, 16, 768), BF16),
            pltpu.VMEM((NX, 2, 16, 768), BF16),
            pltpu.VMEM((NZ, 16, 768), BF16),
            pltpu.VMEM((NZ, 16, 768), BF16),
            pltpu.VMEM((768, 768), BF16),
            pltpu.VMEM((768, 768), BF16),
            dma((2,)),
            dma((2,)),
            *sem(NZ), *sem(NZ), *sem(2, NZ),
            *sem(NX, 2), *sem(NY),
            *sem(NY), *sem(NY, NX),
            *sem(NX), *sem(NX), *sem(NZ),
        ],
        compiler_params=pltpu.CompilerParams(
            collective_id=0, has_side_effects=True, vmem_limit_bytes=48 * 2**20
        ),
    )(tokens, cotangent, weight_in, weight_out)


def solution(mesh):
    return jax.shard_map(
        shards,
        mesh=mesh,
        in_specs=(P("col", "row"), P("col", "row"), P("row", "col"), P("col", "row")),
        out_specs=(P("col", "row"), P("col", "row"), P("row", "col"), P("col", "row")),
        check_vma=False,
    )
```

```python
import jax
import jax.numpy as jnp
from jax import lax
from jax.experimental import pallas as pl
from jax.experimental.pallas import tpu as pltpu
from jax.sharding import PartitionSpec as P

MESH = pl.DeviceIdType.MESH
BF16, F32 = jnp.bfloat16, jnp.float32
NX, NY, NP, NZ, NK = 4, 4, 2, 8, 2
NS = 2
WIDTH, HALF = 768, 384
Z_ORDER = (4, 3, 5, 1, 7, 2, 6)


def gelu_parts(pre_act):
    normal_cdf = 0.5 * (1.0 + jax.scipy.special.erf(pre_act * 0.7071067811865476))
    density = jnp.exp(-0.5 * pre_act * pre_act) * 0.3989422804014327
    return pre_act * normal_cdf, normal_cdf + pre_act * density


def dot(left, right, dims):
    return lax.dot_general(left, right, (dims, ((), ())), preferred_element_type=F32)


def fold(rows):
    return jnp.concatenate([rows[:, :HALF], rows[:, HALF:]], axis=0)


def unfold(block):
    return jnp.concatenate([block[:8], block[8:]], axis=1)


def kernel(
    tok_hbm, cot_hbm, wi_hbm, wo_hbm,
    mixed_ref, gt_ref, gi, go,
    weights, first, gat, rows, own, xs, xr, ys, yr, slopes, act,
    part, ss, sr, ps, pr, zs, zr,
    w_sem,
    az_s, az_r, ay_s, ay_r, ak_s, ak_r,
    rx_s, rx_r, ry_s, ry_r,
    cy_s, cy_r, cx_s, cx_r,
    dk_s, dk_r, dy_s, dy_r, dz_s, dz_r,
):
    r, c = lax.axis_index("row"), lax.axis_index("col")
    yh, x = r // NX, lax.rem(r, NX)
    p, z, k = c // (NZ * NK), lax.rem(c // NK, NZ), lax.rem(c, NK)
    nk, np_ = 1 - k, 1 - p

    def col_dev(p_, z_, k_):
        return (r, p_ * (NZ * NK) + z_ * NK + k_)

    def row_dev(yh_, x_):
        return (yh_ * NX + x_, c)

    def add(a, d, n):
        return lax.rem(a + d + n, n)

    x_dev = [row_dev(yh, add(x, d, NX)) for d in range(NX)]
    y_dev = [row_dev(add(yh, d, NY), x) for d in range(NY)]
    z_dev = [col_dev(p, add(z, d, NZ), k) for d in range(NZ)]
    p_dev, k_dev = col_dev(np_, z, k), col_dev(p, z, nk)

    def copy(src, dst, s_sem, r_sem, device):
        return pltpu.make_async_remote_copy(
            src_ref=src, dst_ref=dst, send_sem=s_sem, recv_sem=r_sem,
            device_id=device, device_id_type=MESH,
        )

    sends = []

    def start(*args):
        one = copy(*args)
        one.start()
        sends.append(one)

    loads = [
        pltpu.make_async_copy(src, dst, w_sem.at[n])
        for n, (src, dst) in enumerate(
            ((tok_hbm, first.at[0]), (cot_hbm, first.at[1]), (wi_hbm, weights.at[0]), (wo_hbm, weights.at[1]))
        )
    ]
    for one in loads:
        one.start()

    peers = x_dev[1:] + y_dev[1:] + z_dev[1:] + [p_dev, k_dev]
    barrier = pltpu.get_barrier_semaphore()
    for peer in peers:
        pl.semaphore_signal(barrier, inc=1, device_id=peer, device_id_type=MESH)
    q_me = p * NZ + z
    for f in range(NS):
        loads[f].wait()
        gat[f, k, q_me] = fold(first[f].astype(F32)).astype(BF16)
    pl.semaphore_wait(barrier, len(peers))

    def gat_at(f, k_, p_, d):
        return gat.at[f, k_, p_ * NZ + add(z, -d, NZ)]

    def forward(f, d):
        blk = gat_at(f, k, p, d)
        if d:
            copy(blk, blk, az_s.at[f, d], az_r.at[f, d], z_dev[d]).wait_recv()
        start(blk, blk, ay_s.at[f, d], ay_r.at[f, d], p_dev)
        start(blk, blk, ak_s.at[f, 0, d], ak_r.at[f, 0, d], k_dev)

    def forward_pair(f, d):
        blk = gat_at(f, k, np_, d)
        copy(blk, blk, ay_s.at[f, d], ay_r.at[f, d], p_dev).wait_recv()
        start(blk, blk, ak_s.at[f, 1, d], ak_r.at[f, 1, d], k_dev)

    def row_terms(f, d0):
        for d in (d0, d0 + 4):
            for side, p_ in ((0, p), (1, np_)):
                blk = gat_at(f, nk, p_, d)
                copy(blk, blk, ak_s.at[f, side, d], ak_r.at[f, side, d], k_dev).wait_recv()
        xt = add(z, -d0, NX)
        for j in range(NY):
            q = j * NX + xt
            both = [unfold(gat[f, i, q].astype(F32)) for i in range(NK)]
            rows[f, xt, pl.ds(16 * j, 16), :] = jnp.concatenate(both, 0).astype(BF16)
        term = dot(rows[f, xt], weights[f], ((1,), (f,)))
        dx = add(xt, -x, NX)

        @pl.when(dx == 0)
        def _():
            own[f] = term.reshape(NY, 16, WIDTH)

        @pl.when(dx != 0)
        def _():
            xs[f, xt] = term.astype(BF16).reshape(NY, 16, WIDTH)
            copy(
                xs.at[f, xt], xr.at[f, dx], rx_s.at[f, dx], rx_r.at[f, dx], row_dev(yh, xt)
            ).start()

    for f in range(NS):
        mine = gat.at[f, k, q_me]
        for d in Z_ORDER:
            start(mine, mine, az_s.at[f, d], az_r.at[f, d], z_dev[d])
        forward(f, 0)
    for d in Z_ORDER:
        forward(0, d)
    forward_pair(0, 0)
    for d in Z_ORDER:
        forward_pair(0, d)
        forward(1, d)
    loads[2].wait()
    row_terms(0, 0)
    forward_pair(1, 0)
    forward_pair(1, 4)
    row_terms(0, 3)
    forward_pair(1, 3)
    forward_pair(1, 5)
    row_terms(0, 1)
    forward_pair(1, 1)
    forward_pair(1, 7)
    row_terms(0, 2)
    forward_pair(1, 2)
    forward_pair(1, 6)
    loads[3].wait()
    for d in (0, 3, 1, 2):
        row_terms(1, d)

    def x_sums(f):
        for d in range(1, NX):
            one = copy(xs.at[f, 0], xr.at[f, d], rx_s.at[f, d], rx_r.at[f, d], x_dev[d])
            one.wait_recv()
            one.wait_send()

        def total(j):
            return own[f, j] + sum(xr[f, d, j].astype(F32) for d in range(1, NX))

        for d in (2, 1, 3):
            ys[f, d] = total(add(yh, d, NY)).astype(BF16)
            start(ys.at[f, d], yr.at[f, d], ry_s.at[f, d], ry_r.at[f, d], y_dev[d])
        own[f, yh] = total(yh)

    def y_sums(f):
        total = own[f, yh]
        for d in (1, 3, 2):
            copy(ys.at[f, d], yr.at[f, d], ry_s.at[f, d], ry_r.at[f, d], y_dev[d]).wait_recv()
            total = total + yr[f, d].astype(F32)
        return total

    def spread(f):
        mine = act.at[f, x, yh]
        for d in (2, 1, 3):
            start(mine, mine, cy_s.at[f, d], cy_r.at[f, d], y_dev[d])
        for e in (2, 1, 3):
            start(mine, mine, cx_s.at[f, 0, e], cx_r.at[f, 0, e], x_dev[e])

    def spread_on(f):
        for d in (1, 3, 2):
            blk = act.at[f, x, add(yh, -d, NY)]
            copy(blk, blk, cy_s.at[f, d], cy_r.at[f, d], y_dev[d]).wait_recv()
            for e in (2, 1, 3):
                start(blk, blk, cx_s.at[f, d, e], cx_r.at[f, d, e], x_dev[e])

    x_sums(0)
    value, slope = gelu_parts(y_sums(0))
    act[0, x, yh] = value.astype(BF16)
    spread(0)
    slopes[...] = slope
    x_sums(1)
    spread_on(0)
    act[1, x, yh] = (y_sums(1) * slopes[...]).astype(BF16)
    spread(1)

    def unit_terms(f, e):
        xt = add(x, -e, NX)
        if e:
            for d in (0, 1, 3, 2):
                blk = act.at[f, xt, add(yh, -d, NY)]
                copy(blk, blk, cx_s.at[f, d, e], cx_r.at[f, d, e], x_dev[e]).wait_recv()
        term = dot(act[f, xt].reshape(64, WIDTH), weights[1 - f], ((1,), (f,)))
        for j in range(NY):
            two = [fold(term[16 * j + 8 * i:16 * j + 8 * i + 8]) for i in range(NK)]
            part[f, e, j] = jnp.where(k == 0, two[0], two[1])
            ss[f, e, j] = jnp.where(k == 0, two[1], two[0])
        start(ss.at[f, e], sr.at[f, e], dk_s.at[f, e], dk_r.at[f, e], k_dev)

    def core_sums(f, e):
        copy(ss.at[f, e], sr.at[f, e], dk_s.at[f, e], dk_r.at[f, e], k_dev).wait_recv()
        for i in range(2):
            j = 2 * np_ + i
            ps[f, e, i] = (part[f, e, j] + sr[f, e, j]).astype(BF16)
        start(ps.at[f, e], pr.at[f, e], dy_s.at[f, e], dy_r.at[f, e], p_dev)

    def pair_sums(f, e):
        copy(ps.at[f, e], pr.at[f, e], dy_s.at[f, e], dy_r.at[f, e], p_dev).wait_recv()
        for i in range(2):
            j = 2 * p + i
            zt = NX * i + add(x, -e, NX)
            total = part[f, e, j] + sr[f, e, j] + pr[f, e, i].astype(F32)
            dz = add(zt, -z, NZ)

            @pl.when(dz == 0)
            def _():
                part[f, 0, 2 * np_] = total

            @pl.when(dz != 0)
            def _():
                zs[f, dz] = total.astype(BF16)
                copy(
                    zs.at[f, dz], zr.at[f, dz], dz_s.at[f, dz], dz_r.at[f, dz], col_dev(p, zt, k)
                ).start()

    def z_sums(f, out):
        total = part[f, 0, 2 * np_]
        for d in range(1, NZ):
            one = copy(zs.at[f, d], zr.at[f, d], dz_s.at[f, d], dz_r.at[f, d], z_dev[d])
            one.wait_recv()
            one.wait_send()
            total = total + zr[f, d].astype(F32)
        out[...] = unfold(total).astype(BF16)

    def grad(left, right, out):
        for m in range(3):
            cols = slice(256 * m, 256 * m + 256)
            out[:, cols] = dot(left, right[:, cols], ((0,), (0,))).astype(BF16)

    order = (0, 1, 3, 2)
    for e in order:
        unit_terms(0, e)
    spread_on(1)
    for e in order:
        core_sums(0, e)
    grad(act[0].reshape(256, WIDTH), rows[1].reshape(256, WIDTH), go)
    for e in order:
        unit_terms(1, e)
    for e in order:
        pair_sums(0, e)
    for e in order:
        core_sums(1, e)
    grad(rows[0].reshape(256, WIDTH), act[1].reshape(256, WIDTH), gi)
    for e in order:
        pair_sums(1, e)
    z_sums(0, mixed_ref)
    z_sums(1, gt_ref)

    for one in sends:
        one.wait_send()


def write_out(*refs):
    sems = refs[-1]
    copies = [pltpu.make_async_copy(refs[i], refs[4 + i], sems.at[i]) for i in range(4)]
    for one in copies:
        one.start()
    for one in copies:
        one.wait()


def shards(tokens, cotangent, weight_in, weight_out):
    dma = pltpu.SemaphoreType.DMA
    vmem, anywhere = pl.BlockSpec(memory_space=pltpu.VMEM), pl.BlockSpec(memory_space=pl.ANY)
    shape = lambda a: jax.ShapeDtypeStruct(a.shape, BF16)
    sem = lambda *n: [dma(n), dma(n)]
    outs = pl.pallas_call(
        kernel,
        out_shape=(shape(tokens), shape(tokens), shape(weight_in), shape(weight_out)),
        in_specs=[anywhere] * 4,
        out_specs=(vmem,) * 4,
        scratch_shapes=[
            pltpu.VMEM((NS, WIDTH, WIDTH), BF16),
            pltpu.VMEM((NS, 8, WIDTH), BF16),
            pltpu.VMEM((NS, NK, NP * NZ, 16, HALF), BF16),
            pltpu.VMEM((NS, NX, 64, WIDTH), BF16),
            pltpu.VMEM((NS, NY, 16, WIDTH), F32),
            pltpu.VMEM((NS, NX, NY, 16, WIDTH), BF16),
            pltpu.VMEM((NS, NX, NY, 16, WIDTH), BF16),
            pltpu.VMEM((NS, NY, 16, WIDTH), BF16),
            pltpu.VMEM((NS, NY, 16, WIDTH), BF16),
            pltpu.VMEM((16, WIDTH), F32),
            pltpu.VMEM((NS, NX, NY, 16, WIDTH), BF16),
            pltpu.VMEM((NS, NX, NY, 16, HALF), F32),
            pltpu.VMEM((NS, NX, NY, 16, HALF), F32),
            pltpu.VMEM((NS, NX, NY, 16, HALF), F32),
            pltpu.VMEM((NS, NX, 2, 16, HALF), BF16),
            pltpu.VMEM((NS, NX, 2, 16, HALF), BF16),
            pltpu.VMEM((NS, NZ, 16, HALF), BF16),
            pltpu.VMEM((NS, NZ, 16, HALF), BF16),
            dma((4,)),
            *sem(NS, NZ), *sem(NS, NZ), *sem(NS, 2, NZ),
            *sem(NS, NX), *sem(NS, NY),
            *sem(NS, NY), *sem(NS, NY, NX),
            *sem(NS, NX), *sem(NS, NX), *sem(NS, NZ),
        ],
        compiler_params=pltpu.CompilerParams(
            collective_id=0, has_side_effects=True, vmem_limit_bytes=51 * 2**20
        ),
    )(tokens, cotangent, weight_in, weight_out)
    return pl.pallas_call(
        write_out,
        out_shape=tuple(shape(a) for a in outs),
        in_specs=[anywhere] * 4,
        out_specs=(anywhere,) * 4,
        scratch_shapes=[dma((4,))],
        compiler_params=pltpu.CompilerParams(vmem_limit_bytes=2**20),
    )(*outs)


def solution(mesh):
    return jax.shard_map(
        shards,
        mesh=mesh,
        in_specs=(P("col", "row"), P("col", "row"), P("row", "col"), P("col", "row")),
        out_specs=(P("col", "row"), P("col", "row"), P("row", "col"), P("col", "row")),
        check_vma=False,
    )
```

```python
import jax
import jax.numpy as jnp
from jax import lax
from jax.experimental import pallas as pl
from jax.experimental.pallas import tpu as pltpu
from jax.sharding import PartitionSpec as P

MESH = pl.DeviceIdType.MESH
BF16, F32 = jnp.bfloat16, jnp.float32
NX, NY, NP, NZ, NK = 4, 4, 2, 8, 2
NS = 2
WIDTH, HALF = 768, 384
Z_ORDER = (0, 4, 3, 7, 5, 1, 2, 6)
SLOT = {d: i for i, d in enumerate(Z_ORDER)}


def gelu_parts(pre_act):
    normal_cdf = 0.5 * (1.0 + jax.scipy.special.erf(pre_act * 0.7071067811865476))
    density = jnp.exp(-0.5 * pre_act * pre_act) * 0.3989422804014327
    return pre_act * normal_cdf, normal_cdf + pre_act * density


def dot(left, right, dims):
    return lax.dot_general(left, right, (dims, ((), ())), preferred_element_type=F32)


def fold(rows):
    return jnp.concatenate([rows[:, :HALF], rows[:, HALF:]], axis=0)


def unfold(block):
    return jnp.concatenate([block[:8], block[8:]], axis=1)


def kernel(
    tok_hbm, cot_hbm, wi_hbm, wo_hbm,
    mixed_ref, gt_ref, gi, go,
    weights, first, gat, rows, own, xs, xr, ys, yr, slopes, act,
    part, ss, sr, ps, pr, zs, zr,
    w_sem,
    az_s, az_r, ay_s, ay_r, ak_s, ak_r,
    rx_s, rx_r, ry_s, ry_r,
    cy_s, cy_r, cx_s, cx_r,
    dk_s, dk_r, dy_s, dy_r, dz_s, dz_r,
):
    r, c = lax.axis_index("row"), lax.axis_index("col")
    yh, x = r // NX, lax.rem(r, NX)
    p, z, k = c // (NZ * NK), lax.rem(c // NK, NZ), lax.rem(c, NK)
    nk, np_ = 1 - k, 1 - p

    def col_dev(p_, z_, k_):
        return (r, p_ * (NZ * NK) + z_ * NK + k_)

    def row_dev(yh_, x_):
        return (yh_ * NX + x_, c)

    def add(a, d, n):
        return lax.rem(a + d + n, n)

    x_dev = [row_dev(yh, add(x, d, NX)) for d in range(NX)]
    y_dev = [row_dev(add(yh, d, NY), x) for d in range(NY)]
    z_dev = [col_dev(p, add(z, d, NZ), k) for d in range(NZ)]
    p_dev, k_dev = col_dev(np_, z, k), col_dev(p, z, nk)

    def copy(src, dst, s_sem, r_sem, device):
        return pltpu.make_async_remote_copy(
            src_ref=src, dst_ref=dst, send_sem=s_sem, recv_sem=r_sem,
            device_id=device, device_id_type=MESH,
        )

    sends = []

    def start(*args):
        one = copy(*args)
        one.start()
        sends.append(one)

    loads = [
        pltpu.make_async_copy(src, dst, w_sem.at[n])
        for n, (src, dst) in enumerate(
            ((tok_hbm, first.at[0]), (cot_hbm, first.at[1]), (wi_hbm, weights.at[0]), (wo_hbm, weights.at[1]))
        )
    ]
    for one in loads:
        one.start()

    peers = x_dev[1:] + y_dev[1:] + z_dev[1:] + [p_dev, k_dev]
    barrier = pltpu.get_barrier_semaphore()
    for peer in peers:
        pl.semaphore_signal(barrier, inc=1, device_id=peer, device_id_type=MESH)
    for f in range(NS):
        loads[f].wait()
        gat[f, k, p, 0] = fold(first[f].astype(F32)).astype(BF16)
    pl.semaphore_wait(barrier, len(peers))

    for f in range(NS):
        for d in Z_ORDER[1:]:
            start(
                gat.at[f, k, p, 0], gat.at[f, k, p, SLOT[d]],
                az_s.at[f, d], az_r.at[f, d], z_dev[d],
            )

    def half(f, k_, p_, h):
        return gat.at[f, k_, p_, pl.ds(4 * h, 4)]

    def forward(f, h):
        for d in Z_ORDER[4 * h:4 * h + 4]:
            if d:
                blk = gat.at[f, k, p, SLOT[d]]
                copy(blk, blk, az_s.at[f, d], az_r.at[f, d], z_dev[d]).wait_recv()
        blk = half(f, k, p, h)
        start(blk, blk, ay_s.at[f, h], ay_r.at[f, h], p_dev)
        start(blk, blk, ak_s.at[f, 0, h], ak_r.at[f, 0, h], k_dev)

    def forward_pair(f, h):
        blk = half(f, k, np_, h)
        copy(blk, blk, ay_s.at[f, h], ay_r.at[f, h], p_dev).wait_recv()
        start(blk, blk, ak_s.at[f, 1, h], ak_r.at[f, 1, h], k_dev)

    def core_arrived(f, h):
        for side, p_ in ((0, p), (1, np_)):
            blk = half(f, nk, p_, h)
            copy(blk, blk, ak_s.at[f, side, h], ak_r.at[f, side, h], k_dev).wait_recv()

    def row_terms(f, d0):
        xt = lax.rem(z - d0 + NZ, NX)
        for d in (d0, d0 + 4):
            high = add(z, -d, NZ) // NX
            for p_ in range(NP):
                both = [unfold(gat[f, i, p_, SLOT[d]].astype(F32)) for i in range(NK)]
                rows[f, xt, 2 * p_ + high] = jnp.concatenate(both, 0).astype(BF16)
        term = dot(rows[f, xt].reshape(64, WIDTH), weights[f], ((1,), (f,)))
        dx = add(xt, -x, NX)

        @pl.when(dx == 0)
        def _():
            own[f] = term.reshape(NY, 16, WIDTH)

        @pl.when(dx != 0)
        def _():
            xs[f, xt] = term.astype(BF16).reshape(NY, 16, WIDTH)
            copy(
                xs.at[f, xt], xr.at[f, dx], rx_s.at[f, dx], rx_r.at[f, dx], row_dev(yh, xt)
            ).start()

    forward(0, 0)
    forward(0, 1)
    forward_pair(0, 0)
    forward(1, 0)
    loads[2].wait()
    core_arrived(0, 0)
    row_terms(0, 0)
    forward_pair(0, 1)
    row_terms(0, 3)
    forward(1, 1)
    core_arrived(0, 1)
    row_terms(0, 1)
    row_terms(0, 2)
    forward_pair(1, 0)
    forward_pair(1, 1)
    loads[3].wait()
    core_arrived(1, 0)
    row_terms(1, 0)
    row_terms(1, 3)
    core_arrived(1, 1)
    row_terms(1, 1)
    row_terms(1, 2)

    def x_sums(f):
        for d in range(1, NX):
            one = copy(xs.at[f, 0], xr.at[f, d], rx_s.at[f, d], rx_r.at[f, d], x_dev[d])
            one.wait_recv()
            one.wait_send()

        def total(j):
            return own[f, j] + sum(xr[f, d, j].astype(F32) for d in range(1, NX))

        for d in (2, 1, 3):
            ys[f, d] = total(add(yh, d, NY)).astype(BF16)
            start(ys.at[f, d], yr.at[f, d], ry_s.at[f, d], ry_r.at[f, d], y_dev[d])
        own[f, yh] = total(yh)

    def y_sums(f):
        total = own[f, yh]
        for d in (1, 3, 2):
            copy(ys.at[f, d], yr.at[f, d], ry_s.at[f, d], ry_r.at[f, d], y_dev[d]).wait_recv()
            total = total + yr[f, d].astype(F32)
        return total

    def spread(f):
        mine = act.at[f, x, yh]
        for d in (2, 1, 3):
            start(mine, mine, cy_s.at[f, d], cy_r.at[f, d], y_dev[d])
        for e in (2, 1, 3):
            start(mine, mine, cx_s.at[f, 0, e], cx_r.at[f, e], x_dev[e])

    def spread_on(f):
        for d in (1, 3, 2):
            blk = act.at[f, x, add(yh, -d, NY)]
            copy(blk, blk, cy_s.at[f, d], cy_r.at[f, d], y_dev[d]).wait_recv()
            for e in (2, 1, 3):
                start(blk, blk, cx_s.at[f, d, e], cx_r.at[f, e], x_dev[e])

    x_sums(0)
    value, slope = gelu_parts(y_sums(0))
    act[0, x, yh] = value.astype(BF16)
    spread(0)
    slopes[...] = slope
    x_sums(1)
    spread_on(0)
    act[1, x, yh] = (y_sums(1) * slopes[...]).astype(BF16)
    spread(1)

    def unit_terms(f, e):
        xt = add(x, -e, NX)
        if e:
            blk = act.at[f, xt]
            copy(blk, blk, cx_s.at[f, 0, e], cx_r.at[f, e], x_dev[e]).wait_recv()
        term = dot(act[f, xt].reshape(64, WIDTH), weights[1 - f], ((1,), (f,)))
        for j in range(NY):
            two = [fold(term[16 * j + 8 * i:16 * j + 8 * i + 8]) for i in range(NK)]
            part[f, e, j] = jnp.where(k == 0, two[0], two[1])
            ss[f, e, j] = jnp.where(k == 0, two[1], two[0])
        start(ss.at[f, e], sr.at[f, e], dk_s.at[f, e], dk_r.at[f, e], k_dev)

    def core_sums(f, e):
        copy(ss.at[f, e], sr.at[f, e], dk_s.at[f, e], dk_r.at[f, e], k_dev).wait_recv()
        for i in range(2):
            j = 2 * np_ + i
            ps[f, e, i] = (part[f, e, j] + sr[f, e, j]).astype(BF16)
        start(ps.at[f, e], pr.at[f, e], dy_s.at[f, e], dy_r.at[f, e], p_dev)

    def pair_sums(f, e):
        copy(ps.at[f, e], pr.at[f, e], dy_s.at[f, e], dy_r.at[f, e], p_dev).wait_recv()
        for i in range(2):
            j = 2 * p + i
            zt = NX * i + add(x, -e, NX)
            total = part[f, e, j] + sr[f, e, j] + pr[f, e, i].astype(F32)
            dz = add(zt, -z, NZ)

            @pl.when(dz == 0)
            def _():
                part[f, 0, 2 * np_] = total

            @pl.when(dz != 0)
            def _():
                zs[f, dz] = total.astype(BF16)
                copy(
                    zs.at[f, dz], zr.at[f, dz], dz_s.at[f, dz], dz_r.at[f, dz], col_dev(p, zt, k)
                ).start()

    def z_sums(f, out):
        total = part[f, 0, 2 * np_]
        for d in range(1, NZ):
            one = copy(zs.at[f, d], zr.at[f, d], dz_s.at[f, d], dz_r.at[f, d], z_dev[d])
            one.wait_recv()
            one.wait_send()
            total = total + zr[f, d].astype(F32)
        out[...] = unfold(total).astype(BF16)

    def grad(left, right, out):
        for m in range(3):
            cols = slice(256 * m, 256 * m + 256)
            out[:, cols] = dot(left, right[:, cols], ((0,), (0,))).astype(BF16)

    def drain():
        for one in sends:
            one.wait_send()

    order = (0, 1, 3, 2)
    for e in order:
        unit_terms(0, e)
    spread_on(1)
    for e in order:
        core_sums(0, e)
    grad(act[0].reshape(256, WIDTH), rows[1].reshape(256, WIDTH), go)
    for e in order:
        unit_terms(1, e)
    for e in order:
        pair_sums(0, e)
    for e in order:
        core_sums(1, e)
    grad(rows[0].reshape(256, WIDTH), act[1].reshape(256, WIDTH), gi)
    drain()
    for e in order:
        pair_sums(1, e)
    z_sums(0, mixed_ref)
    z_sums(1, gt_ref)


def write_out(*refs):
    sems = refs[-1]
    copies = [pltpu.make_async_copy(refs[i], refs[4 + i], sems.at[i]) for i in range(4)]
    for one in copies:
        one.start()
    for one in copies:
        one.wait()


def shards(tokens, cotangent, weight_in, weight_out):
    dma = pltpu.SemaphoreType.DMA
    vmem, anywhere = pl.BlockSpec(memory_space=pltpu.VMEM), pl.BlockSpec(memory_space=pl.ANY)
    shape = lambda a: jax.ShapeDtypeStruct(a.shape, BF16)
    sem = lambda *n: [dma(n), dma(n)]
    outs = pl.pallas_call(
        kernel,
        out_shape=(shape(tokens), shape(tokens), shape(weight_in), shape(weight_out)),
        in_specs=[anywhere] * 4,
        out_specs=(vmem,) * 4,
        scratch_shapes=[
            pltpu.VMEM((NS, WIDTH, WIDTH), BF16),
            pltpu.VMEM((NS, 8, WIDTH), BF16),
            pltpu.VMEM((NS, NK, NP, NZ, 16, HALF), BF16),
            pltpu.VMEM((NS, NX, NY, 16, WIDTH), BF16),
            pltpu.VMEM((NS, NY, 16, WIDTH), F32),
            pltpu.VMEM((NS, NX, NY, 16, WIDTH), BF16),
            pltpu.VMEM((NS, NX, NY, 16, WIDTH), BF16),
            pltpu.VMEM((NS, NY, 16, WIDTH), BF16),
            pltpu.VMEM((NS, NY, 16, WIDTH), BF16),
            pltpu.VMEM((16, WIDTH), F32),
            pltpu.VMEM((NS, NX, NY, 16, WIDTH), BF16),
            pltpu.VMEM((NS, NX, NY, 16, HALF), F32),
            pltpu.VMEM((NS, NX, NY, 16, HALF), F32),
            pltpu.VMEM((NS, NX, NY, 16, HALF), F32),
            pltpu.VMEM((NS, NX, 2, 16, HALF), BF16),
            pltpu.VMEM((NS, NX, 2, 16, HALF), BF16),
            pltpu.VMEM((NS, NZ, 16, HALF), BF16),
            pltpu.VMEM((NS, NZ, 16, HALF), BF16),
            dma((4,)),
            *sem(NS, NZ), *sem(NS, 2), *sem(NS, 2, 2),
            *sem(NS, NX), *sem(NS, NY),
            *sem(NS, NY), dma((NS, NY, NX)), dma((NS, NX)),
            *sem(NS, NX), *sem(NS, NX), *sem(NS, NZ),
        ],
        compiler_params=pltpu.CompilerParams(
            collective_id=0, has_side_effects=True, vmem_limit_bytes=51 * 2**20
        ),
    )(tokens, cotangent, weight_in, weight_out)
    return pl.pallas_call(
        write_out,
        out_shape=tuple(shape(a) for a in outs),
        in_specs=[anywhere] * 4,
        out_specs=(anywhere,) * 4,
        scratch_shapes=[dma((4,))],
        compiler_params=pltpu.CompilerParams(vmem_limit_bytes=2**20),
    )(*outs)


def solution(mesh):
    return jax.shard_map(
        shards,
        mesh=mesh,
        in_specs=(P("col", "row"), P("col", "row"), P("row", "col"), P("col", "row")),
        out_specs=(P("col", "row"), P("col", "row"), P("row", "col"), P("col", "row")),
        check_vma=False,
    )
```

```python
import jax
import jax.numpy as jnp
from jax import lax
from jax.experimental import pallas as pl
from jax.experimental.pallas import tpu as pltpu
from jax.sharding import PartitionSpec as P

MESH = pl.DeviceIdType.MESH
BF16, F32 = jnp.bfloat16, jnp.float32
NX, NY, NP, NZ, NK = 4, 4, 2, 8, 2
NS = 2
WIDTH, HALF = 768, 384
Z_ORDER = (0, 4, 3, 7, 5, 1, 2, 6)
SLOT = {d: i for i, d in enumerate(Z_ORDER)}


def gelu_parts(pre_act):
    normal_cdf = 0.5 * (1.0 + jax.scipy.special.erf(pre_act * 0.7071067811865476))
    density = jnp.exp(-0.5 * pre_act * pre_act) * 0.3989422804014327
    return pre_act * normal_cdf, normal_cdf + pre_act * density


def dot(left, right, dims):
    return lax.dot_general(left, right, (dims, ((), ())), preferred_element_type=F32)


def fold(rows):
    return jnp.concatenate([rows[:, :HALF], rows[:, HALF:]], axis=0)


def unfold(block):
    return jnp.concatenate([block[:8], block[8:]], axis=1)


def kernel(
    tok_ref, cot_ref, wi_hbm, wo_hbm,
    mixed_ref, gt_ref, gi, go,
    weights, gat, rows, own, xs, xr, ys, yr, slopes, act,
    part, ss, sr, ps, pr, zs, zr,
    w_sem,
    az_s, az_r, ay_s, ay_r, ak_s, ak_r,
    rx_s, rx_r, ry_s, ry_r,
    cy_s, cy_r, cx_s, cx_r,
    dk_s, dk_r, dy_s, dy_r, dz_s, dz_r,
):
    r, c = lax.axis_index("row"), lax.axis_index("col")
    yh, x = r // NX, lax.rem(r, NX)
    p, z, k = c // (NZ * NK), lax.rem(c // NK, NZ), lax.rem(c, NK)
    nk, np_ = 1 - k, 1 - p

    def col_dev(p_, z_, k_):
        return (r, p_ * (NZ * NK) + z_ * NK + k_)

    def row_dev(yh_, x_):
        return (yh_ * NX + x_, c)

    def add(a, d, n):
        return lax.rem(a + d + n, n)

    x_dev = [row_dev(yh, add(x, d, NX)) for d in range(NX)]
    y_dev = [row_dev(add(yh, d, NY), x) for d in range(NY)]
    z_dev = [col_dev(p, add(z, d, NZ), k) for d in range(NZ)]
    p_dev, k_dev = col_dev(np_, z, k), col_dev(p, z, nk)

    def copy(src, dst, s_sem, r_sem, device):
        return pltpu.make_async_remote_copy(
            src_ref=src, dst_ref=dst, send_sem=s_sem, recv_sem=r_sem,
            device_id=device, device_id_type=MESH,
        )

    sends = []

    def start(*args):
        one = copy(*args)
        one.start()
        sends.append(one)

    loads = [
        pltpu.make_async_copy(src, dst, w_sem.at[n])
        for n, (src, dst) in enumerate(
            ((wi_hbm, weights.at[0]), (wo_hbm, weights.at[1]))
        )
    ]
    for one in loads:
        one.start()

    peers = x_dev[1:] + y_dev[1:] + z_dev[1:] + [p_dev, k_dev]
    barrier = pltpu.get_barrier_semaphore()
    for peer in peers:
        pl.semaphore_signal(barrier, inc=1, device_id=peer, device_id_type=MESH)
    for f in range(NS):
        gat[f, k, p, 0] = fold((tok_ref, cot_ref)[f][...].astype(F32)).astype(BF16)
    pl.semaphore_wait(barrier, len(peers))

    for f in range(NS):
        for d in Z_ORDER[1:]:
            start(
                gat.at[f, k, p, 0], gat.at[f, k, p, SLOT[d]],
                az_s.at[f, d], az_r.at[f, d], z_dev[d],
            )

    def half(f, k_, p_, h):
        return gat.at[f, k_, p_, pl.ds(4 * h, 4)]

    def forward(f, h):
        for d in Z_ORDER[4 * h:4 * h + 4]:
            if d:
                blk = gat.at[f, k, p, SLOT[d]]
                copy(blk, blk, az_s.at[f, d], az_r.at[f, d], z_dev[d]).wait_recv()
        blk = half(f, k, p, h)
        start(blk, blk, ay_s.at[f, h], ay_r.at[f, h], p_dev)
        start(blk, blk, ak_s.at[f, 0, h], ak_r.at[f, 0, h], k_dev)

    def forward_pair(f, h):
        blk = half(f, k, np_, h)
        copy(blk, blk, ay_s.at[f, h], ay_r.at[f, h], p_dev).wait_recv()
        start(blk, blk, ak_s.at[f, 1, h], ak_r.at[f, 1, h], k_dev)

    def core_arrived(f, h):
        for side, p_ in ((0, p), (1, np_)):
            blk = half(f, nk, p_, h)
            copy(blk, blk, ak_s.at[f, side, h], ak_r.at[f, side, h], k_dev).wait_recv()

    def row_terms(f, d0):
        xt = lax.rem(z - d0 + NZ, NX)
        for d in (d0, d0 + 4):
            high = add(z, -d, NZ) // NX
            for p_ in range(NP):
                both = [unfold(gat[f, i, p_, SLOT[d]].astype(F32)) for i in range(NK)]
                rows[f, xt, 2 * p_ + high] = jnp.concatenate(both, 0).astype(BF16)
        term = dot(rows[f, xt].reshape(64, WIDTH), weights[f], ((1,), (f,)))
        dx = add(xt, -x, NX)

        @pl.when(dx == 0)
        def _():
            own[f] = term.reshape(NY, 16, WIDTH)

        @pl.when(dx != 0)
        def _():
            xs[f, xt] = term.astype(BF16).reshape(NY, 16, WIDTH)
            copy(
                xs.at[f, xt], xr.at[f, dx], rx_s.at[f, dx], rx_r.at[f, dx], row_dev(yh, xt)
            ).start()

    forward(0, 0)
    forward(0, 1)
    forward_pair(0, 0)
    forward(1, 0)
    loads[0].wait()
    core_arrived(0, 0)
    row_terms(0, 0)
    forward_pair(0, 1)
    row_terms(0, 3)
    forward(1, 1)
    core_arrived(0, 1)
    row_terms(0, 1)
    row_terms(0, 2)
    forward_pair(1, 0)
    forward_pair(1, 1)
    loads[1].wait()
    core_arrived(1, 0)
    row_terms(1, 0)
    row_terms(1, 3)
    core_arrived(1, 1)
    row_terms(1, 1)
    row_terms(1, 2)

    def x_sums(f):
        for d in range(1, NX):
            one = copy(xs.at[f, 0], xr.at[f, d], rx_s.at[f, d], rx_r.at[f, d], x_dev[d])
            one.wait_recv()
            one.wait_send()

        def total(j):
            return own[f, j] + sum(xr[f, d, j].astype(F32) for d in range(1, NX))

        for d in (2, 1, 3):
            ys[f, d] = total(add(yh, d, NY)).astype(BF16)
            start(ys.at[f, d], yr.at[f, d], ry_s.at[f, d], ry_r.at[f, d], y_dev[d])
        own[f, yh] = total(yh)

    def y_sums(f):
        total = own[f, yh]
        for d in (1, 3, 2):
            copy(ys.at[f, d], yr.at[f, d], ry_s.at[f, d], ry_r.at[f, d], y_dev[d]).wait_recv()
            total = total + yr[f, d].astype(F32)
        return total

    def spread(f):
        mine = act.at[f, x, yh]
        for d in (2, 1, 3):
            start(mine, mine, cy_s.at[f, d], cy_r.at[f, d], y_dev[d])
        for e in (2, 1, 3):
            start(mine, mine, cx_s.at[f, 0, e], cx_r.at[f, e], x_dev[e])

    def spread_on(f):
        for d in (1, 3, 2):
            blk = act.at[f, x, add(yh, -d, NY)]
            copy(blk, blk, cy_s.at[f, d], cy_r.at[f, d], y_dev[d]).wait_recv()
            for e in (2, 1, 3):
                start(blk, blk, cx_s.at[f, d, e], cx_r.at[f, e], x_dev[e])

    x_sums(0)
    value, slope = gelu_parts(y_sums(0))
    act[0, x, yh] = value.astype(BF16)
    spread(0)
    slopes[...] = slope
    x_sums(1)
    spread_on(0)
    act[1, x, yh] = (y_sums(1) * slopes[...]).astype(BF16)
    spread(1)

    def unit_terms(f, e):
        xt = add(x, -e, NX)
        if e:
            blk = act.at[f, xt]
            copy(blk, blk, cx_s.at[f, 0, e], cx_r.at[f, e], x_dev[e]).wait_recv()
        term = dot(act[f, xt].reshape(64, WIDTH), weights[1 - f], ((1,), (f,)))
        for j in range(NY):
            two = [fold(term[16 * j + 8 * i:16 * j + 8 * i + 8]) for i in range(NK)]
            part[f, e, j] = jnp.where(k == 0, two[0], two[1])
            ss[f, e, j] = jnp.where(k == 0, two[1], two[0])
        start(ss.at[f, e], sr.at[f, e], dk_s.at[f, e], dk_r.at[f, e], k_dev)

    def core_sums(f, e):
        copy(ss.at[f, e], sr.at[f, e], dk_s.at[f, e], dk_r.at[f, e], k_dev).wait_recv()
        for i in range(2):
            j = 2 * np_ + i
            ps[f, e, i] = (part[f, e, j] + sr[f, e, j]).astype(BF16)
        start(ps.at[f, e], pr.at[f, e], dy_s.at[f, e], dy_r.at[f, e], p_dev)

    def pair_sums(f, e):
        copy(ps.at[f, e], pr.at[f, e], dy_s.at[f, e], dy_r.at[f, e], p_dev).wait_recv()
        for i in range(2):
            j = 2 * p + i
            zt = NX * i + add(x, -e, NX)
            total = part[f, e, j] + sr[f, e, j] + pr[f, e, i].astype(F32)
            dz = add(zt, -z, NZ)

            @pl.when(dz == 0)
            def _():
                part[f, 0, 2 * np_] = total

            @pl.when(dz != 0)
            def _():
                zs[f, dz] = total.astype(BF16)
                copy(
                    zs.at[f, dz], zr.at[f, dz], dz_s.at[f, dz], dz_r.at[f, dz], col_dev(p, zt, k)
                ).start()

    def z_sums(f, out):
        total = part[f, 0, 2 * np_]
        for d in range(1, NZ):
            one = copy(zs.at[f, d], zr.at[f, d], dz_s.at[f, d], dz_r.at[f, d], z_dev[d])
            one.wait_recv()
            one.wait_send()
            total = total + zr[f, d].astype(F32)
        out[...] = unfold(total).astype(BF16)

    def grad(left, right, out):
        for m in range(3):
            cols = slice(256 * m, 256 * m + 256)
            out[:, cols] = dot(left, right[:, cols], ((0,), (0,))).astype(BF16)

    def drain():
        for one in sends:
            one.wait_send()

    order = (0, 1, 3, 2)
    for e in order:
        unit_terms(0, e)
    spread_on(1)
    for e in order:
        core_sums(0, e)
    grad(act[0].reshape(256, WIDTH), rows[1].reshape(256, WIDTH), go)
    for e in order:
        unit_terms(1, e)
    for e in order:
        pair_sums(0, e)
    for e in order:
        core_sums(1, e)
    grad(rows[0].reshape(256, WIDTH), act[1].reshape(256, WIDTH), gi)
    drain()
    for e in order:
        pair_sums(1, e)
    z_sums(0, mixed_ref)
    z_sums(1, gt_ref)


def write_out(mixed, gt, gi, go, mixed_out, gt_out, gi_out, go_out, sems):
    copies = [
        pltpu.make_async_copy(gi, gi_out, sems.at[0]),
        pltpu.make_async_copy(go, go_out, sems.at[1]),
    ]
    for one in copies:
        one.start()
    mixed_out[...] = mixed[...]
    gt_out[...] = gt[...]
    for one in copies:
        one.wait()


def shards(tokens, cotangent, weight_in, weight_out):
    dma = pltpu.SemaphoreType.DMA
    vmem, anywhere = pl.BlockSpec(memory_space=pltpu.VMEM), pl.BlockSpec(memory_space=pl.ANY)
    shape = lambda a: jax.ShapeDtypeStruct(a.shape, BF16)
    sem = lambda *n: [dma(n), dma(n)]
    outs = pl.pallas_call(
        kernel,
        out_shape=(shape(tokens), shape(tokens), shape(weight_in), shape(weight_out)),
        in_specs=[vmem, vmem, anywhere, anywhere],
        out_specs=(vmem,) * 4,
        scratch_shapes=[
            pltpu.VMEM((NS, WIDTH, WIDTH), BF16),
            pltpu.VMEM((NS, NK, NP, NZ, 16, HALF), BF16),
            pltpu.VMEM((NS, NX, NY, 16, WIDTH), BF16),
            pltpu.VMEM((NS, NY, 16, WIDTH), F32),
            pltpu.VMEM((NS, NX, NY, 16, WIDTH), BF16),
            pltpu.VMEM((NS, NX, NY, 16, WIDTH), BF16),
            pltpu.VMEM((NS, NY, 16, WIDTH), BF16),
            pltpu.VMEM((NS, NY, 16, WIDTH), BF16),
            pltpu.VMEM((16, WIDTH), F32),
            pltpu.VMEM((NS, NX, NY, 16, WIDTH), BF16),
            pltpu.VMEM((NS, NX, NY, 16, HALF), F32),
            pltpu.VMEM((NS, NX, NY, 16, HALF), F32),
            pltpu.VMEM((NS, NX, NY, 16, HALF), F32),
            pltpu.VMEM((NS, NX, 2, 16, HALF), BF16),
            pltpu.VMEM((NS, NX, 2, 16, HALF), BF16),
            pltpu.VMEM((NS, NZ, 16, HALF), BF16),
            pltpu.VMEM((NS, NZ, 16, HALF), BF16),
            dma((2,)),
            *sem(NS, NZ), *sem(NS, 2), *sem(NS, 2, 2),
            *sem(NS, NX), *sem(NS, NY),
            *sem(NS, NY), dma((NS, NY, NX)), dma((NS, NX)),
            *sem(NS, NX), *sem(NS, NX), *sem(NS, NZ),
        ],
        compiler_params=pltpu.CompilerParams(
            collective_id=0, has_side_effects=True, vmem_limit_bytes=51 * 2**20
        ),
    )(tokens, cotangent, weight_in, weight_out)
    return pl.pallas_call(
        write_out,
        out_shape=tuple(shape(a) for a in outs),
        in_specs=[vmem, vmem, anywhere, anywhere],
        out_specs=(vmem, vmem, anywhere, anywhere),
        scratch_shapes=[dma((2,))],
        compiler_params=pltpu.CompilerParams(vmem_limit_bytes=2**20),
    )(*outs)


def solution(mesh):
    return jax.shard_map(
        shards,
        mesh=mesh,
        in_specs=(P("col", "row"), P("col", "row"), P("row", "col"), P("col", "row")),
        out_specs=(P("col", "row"), P("col", "row"), P("row", "col"), P("col", "row")),
        check_vma=False,
    )
```
